512 devices in a mesh: dp: 16 (over x, y), vocab: 32 (over z, core).
Axes of the slice: x: 4, y: 4, z: 16, core: 2. Of those that a mesh axis runs over, the one named last changes fastest.
Arguments:
- student_hidden: bfloat16 [6144, 896], P('dp'), may hold values from -1500 to 1500
- head_weight: bfloat16 [896, 77824], P('dp', 'vocab'), may hold values from -0.625 to 0.625
- teacher_logits: bfloat16 [6144, 77824], P('dp', 'vocab'), may hold values from -4400 to 4400
Outputs:
- logit_grad: bfloat16 [6144, 77824], P('dp', 'vocab')
- hidden_grad: bfloat16 [6144, 896], P('dp', 'vocab')
The draws below stay inside these ranges and needn't reach their ends.
All inputs are finite; a program needn't handle non-finite values.
Results may differ from the reference program's by a relative error of at most 0.005.
Values may be sent and summed in bfloat16 or wider, within the bound.
No kernel may reach another device: no remote copies, remote signals or barrier semaphores. Data moves between devices by JAX's collectives and lax.ppermute only.
A program may use at most 64 MiB of HBM per device.

```python
import jax
import jax.numpy as jnp
from jax import lax

D = 896
V_DEV = 2432
TEMP = 4
V = 77824
TOKENS = 6144
N_VOCAB = 32


def draw_student_hidden(key, part):
    first = jax.random.fold_in(jax.random.fold_in(key, 11), 0)
    values = jax.random.truncated_normal(first, -6.0, 6.0, (TOKENS, D), jnp.float32)
    return values.astype(jnp.bfloat16)


def draw_teacher_logits(key, part):
    first = jax.random.fold_in(jax.random.fold_in(key, 23), 0)
    values = 3.0 * jax.random.truncated_normal(first, -6.0, 6.0, (TOKENS, V), jnp.float32)
    position = jnp.arange(V, dtype=jnp.float32) / V
    return (values + TEMP * jnp.log(1.0 + 2.0 * position)[None, :]).astype(jnp.bfloat16)


def block_scale(own_key, extent, cuts, low, largest):
    factor_of, own = 1.0, jax.random.fold_in(own_key, 6)
    for axis_at, blocks in cuts:
        heights = jnp.exp(jax.random.uniform(jax.random.fold_in(own, axis_at), (blocks,), jnp.float32, low / len(cuts), largest / len(cuts)))
        factor_of = factor_of * jnp.repeat(heights, extent[axis_at] // blocks).reshape([-1 if axis == axis_at else 1 for axis in range(len(extent))])
    return factor_of


def bell_draw(key, dims, spread, reach, cuts=(), held_as=jnp.bfloat16):
    values = jax.random.normal(key, dims, jnp.float32) * spread
    if len(cuts) > 0:
        values = block_scale(key, dims, cuts, -0.22, 0.18) * values
    return jnp.clip(values, min=-reach, max=reach).astype(held_as)


def setup_inputs(seed: int = 0) -> dict:
    key_of = jax.random.split(jax.random.key(seed), 4)
    return {
        "student_hidden": draw_student_hidden(jax.random.fold_in(key_of[3], 71), 0),
        "head_weight": bell_draw(key_of[1], (D, V), (D // 9) ** -0.5, 0.625, ((0, 16), (1, 32))),
        "teacher_logits": draw_teacher_logits(jax.random.fold_in(key_of[3], 71), 0),
    }


EPS = 1e-06

def gradient_terms(prob_student, prob_teacher, row_terms, col_terms):
    row_den, row_rho, row_var = row_terms
    mean_s, mean_t, col_var, col_den, col_rho = col_terms
    inner = prob_teacher / row_den[:, None] - (row_rho / (row_var + EPS))[:, None] * prob_student
    inner = inner + (prob_teacher - mean_t[None, :]) / col_den[None, :]
    inner = inner - (col_rho / (col_var + EPS))[None, :] * (prob_student - mean_s[None, :])
    return -TEMP * inner

def reference(student_hidden, head_weight, teacher_logits):
    logits = jnp.dot(student_hidden, head_weight, preferred_element_type=jnp.float32)
    peak_student = lax.optimization_barrier(jnp.max(logits, axis=1)) / TEMP
    peak_teacher = lax.optimization_barrier(jnp.max(teacher_logits.astype(jnp.float32), axis=1)) / TEMP
    blocks = jnp.arange(N_VOCAB, dtype=jnp.int32)

    def exps(index):
        begin = (index * V_DEV).astype(jnp.int32)
        zs = lax.dynamic_slice_in_dim(logits, begin, V_DEV, 1)
        zt = lax.dynamic_slice_in_dim(teacher_logits, begin, V_DEV, 1).astype(jnp.float32)
        return (jnp.exp(zs / TEMP - peak_student[:, None]), jnp.exp(zt / TEMP - peak_teacher[:, None]))

    def row_part(index):
        exp_student, exp_teacher = exps(index)
        return jnp.stack([lax.optimization_barrier(jnp.sum(exp_student, 1)), lax.optimization_barrier(jnp.sum(exp_teacher, 1)), lax.optimization_barrier(jnp.sum(exp_student * exp_student, 1)), lax.optimization_barrier(jnp.sum(exp_teacher * exp_teacher, 1)), lax.optimization_barrier(jnp.sum(exp_student * exp_teacher, 1))])
    moments = lax.optimization_barrier(jnp.sum(lax.map(row_part, blocks), axis=0))
    norm_student, norm_teacher = (moments[0], moments[1])
    row_var = V * moments[2] / (norm_student * norm_student) - 1.0
    row_var_t = V * moments[3] / (norm_teacher * norm_teacher) - 1.0
    cross = V * moments[4] / (norm_student * norm_teacher) - 1.0
    row_den = jnp.sqrt((row_var + EPS) * (row_var_t + EPS))
    row_terms = (row_den, cross / row_den, row_var)

    def probs(index):
        exp_student, exp_teacher = exps(index)
        return (V * exp_student / norm_student[:, None], V * exp_teacher / norm_teacher[:, None])

    def col_part(index):
        prob_student, prob_teacher = probs(index)
        return jnp.stack([lax.optimization_barrier(jnp.sum(prob_student, 0)), lax.optimization_barrier(jnp.sum(prob_teacher, 0)), lax.optimization_barrier(jnp.sum(prob_student * prob_student, 0)), lax.optimization_barrier(jnp.sum(prob_teacher * prob_teacher, 0)), lax.optimization_barrier(jnp.sum(prob_student * prob_teacher, 0))])
    columns = lax.map(col_part, blocks)

    def col_terms(index):
        sums = columns[index]
        mean_s = sums[0] / TOKENS
        mean_t = sums[1] / TOKENS
        col_var = sums[2] / TOKENS - mean_s * mean_s
        col_var_t = sums[3] / TOKENS - mean_t * mean_t
        col_cov = sums[4] / TOKENS - mean_s * mean_t
        col_den = jnp.sqrt((col_var + EPS) * (col_var_t + EPS))
        return (mean_s, mean_t, col_var, col_den, col_cov / col_den)

    def dot_part(index):
        prob_student, prob_teacher = probs(index)
        coeff = gradient_terms(prob_student, prob_teacher, row_terms, col_terms(index))
        return lax.optimization_barrier(jnp.sum(prob_student * coeff, 1))
    row_dot = lax.optimization_barrier(jnp.sum(lax.map(dot_part, blocks), axis=0)) / V

    def grad_part(index):
        prob_student, prob_teacher = probs(index)
        coeff = gradient_terms(prob_student, prob_teacher, row_terms, col_terms(index))
        return (prob_student * (coeff - row_dot[:, None]) / TEMP).astype(jnp.bfloat16)
    pieces = lax.map(grad_part, blocks)
    logit_grad = jnp.transpose(pieces, (1, 0, 2)).reshape(TOKENS, V)
    hidden_grad = jnp.dot(logit_grad, head_weight.T, preferred_element_type=jnp.float32).astype(jnp.bfloat16)
    return (logit_grad, hidden_grad)
```

```python
import jax
import jax.numpy as jnp
from jax import lax
from jax.sharding import PartitionSpec as P

TEMP = 4
EPS = 1e-06
SIDE = 4
CHIPS = 16
CORES = 2
DP = SIDE * SIDE
VOCAB = CHIPS * CORES
AXES = ("dp", "vocab")


def _plane_groups(flip):
    groups = []
    for z in range(CHIPS):
        for core in range(CORES):
            for other in range(SIDE):
                along_x = (core ^ flip) == 0
                groups.append(
                    [
                        ((i * SIDE + other) if along_x else (other * SIDE + i)) * VOCAB + z * CORES + core
                        for i in range(SIDE)
                    ]
                )
    return groups


FIRST, SECOND = _plane_groups(0), _plane_groups(1)
COLUMN = [[z * CORES + core for z in range(CHIPS)] for core in range(CORES)]
PAIR = [(i, i ^ 1) for i in range(VOCAB)]


def spread(block, count, axis, groups=None):
    copies = jnp.broadcast_to(block[None], (count,) + block.shape)
    return lax.all_to_all(copies, axis, 0, 0, tiled=True, axis_index_groups=groups)


def merge(parts):
    peak_s, peak_t = jnp.max(parts[:, 0], 0), jnp.max(parts[:, 1], 0)
    ws, wt = jnp.exp(parts[:, 0] - peak_s), jnp.exp(parts[:, 1] - peak_t)
    return jnp.stack(
        [
            peak_s,
            peak_t,
            jnp.sum(parts[:, 2] * ws, 0),
            jnp.sum(parts[:, 3] * wt, 0),
            jnp.sum(parts[:, 4] * (ws * ws), 0),
            jnp.sum(parts[:, 5] * (wt * wt), 0),
            jnp.sum(parts[:, 6] * (ws * wt), 0),
        ]
    )


def body(student_hidden, head_weight, teacher_logits):
    tok_rows, width = student_hidden.shape
    rows, vocab_cols = head_weight.shape
    classes = vocab_cols * VOCAB
    tokens = tok_rows * DP
    core = lax.axis_index("vocab") % CORES

    line = spread(head_weight, SIDE, AXES, FIRST).reshape(SIDE * rows, vocab_cols)
    whole = spread(line, SIDE, AXES, SECOND).reshape(DP * rows, vocab_cols)
    hid = student_hidden.reshape(tok_rows, SIDE, SIDE, rows)
    hid = jnp.where(core == 0, jnp.swapaxes(hid, 1, 2), hid).reshape(tok_rows, width)

    logits = jnp.dot(hid, whole, preferred_element_type=jnp.float32)
    scaled_student = logits / TEMP
    scaled_teacher = teacher_logits.astype(jnp.float32) / TEMP
    own_s = jnp.max(scaled_student, axis=1)
    own_t = jnp.max(scaled_teacher, axis=1)
    exp_s = jnp.exp(scaled_student - own_s[:, None])
    exp_t = jnp.exp(scaled_teacher - own_t[:, None])
    stats = jnp.stack(
        [
            own_s,
            own_t,
            jnp.sum(exp_s, 1),
            jnp.sum(exp_t, 1),
            jnp.sum(exp_s * exp_s, 1),
            jnp.sum(exp_t * exp_t, 1),
            jnp.sum(exp_s * exp_t, 1),
        ]
    )
    stats = merge(jnp.stack([stats, lax.ppermute(stats, "vocab", PAIR)]))
    stats = merge(spread(stats, CHIPS, "vocab", COLUMN))
    norm_s, norm_t = stats[2], stats[3]
    row_var = classes * stats[4] / (norm_s * norm_s) - 1.0
    row_var_t = classes * stats[5] / (norm_t * norm_t) - 1.0
    cross = classes * stats[6] / (norm_s * norm_t) - 1.0
    row_den = jnp.sqrt((row_var + EPS) * (row_var_t + EPS))
    row_rho = cross / row_den
    prob_s = exp_s * (classes * jnp.exp(own_s - stats[0]) / norm_s)[:, None]
    prob_t = exp_t * (classes * jnp.exp(own_t - stats[1]) / norm_t)[:, None]

    sums = jnp.stack(
        [
            jnp.sum(prob_s, 0),
            jnp.sum(prob_t, 0),
            jnp.sum(prob_s * prob_s, 0),
            jnp.sum(prob_t * prob_t, 0),
            jnp.sum(prob_s * prob_t, 0),
        ]
    )
    sums = jnp.sum(spread(sums, SIDE, AXES, FIRST), 0)
    sums = jnp.sum(spread(sums, SIDE, AXES, SECOND), 0)
    mean_s = sums[0] / tokens
    mean_t = sums[1] / tokens
    col_var = sums[2] / tokens - mean_s * mean_s
    col_var_t = sums[3] / tokens - mean_t * mean_t
    col_cov = sums[4] / tokens - mean_s * mean_t
    col_den = jnp.sqrt((col_var + EPS) * (col_var_t + EPS))
    col_rho = col_cov / col_den

    inner = prob_t / row_den[:, None] - (row_rho / (row_var + EPS))[:, None] * prob_s
    inner = inner + (prob_t - mean_t[None, :]) / col_den[None, :]
    inner = inner - (col_rho / (col_var + EPS))[None, :] * (prob_s - mean_s[None, :])
    coeff = -TEMP * inner
    row_dot = jnp.sum(prob_s * coeff, 1)
    row_dot = jnp.sum(spread(row_dot[None], VOCAB, "vocab"), (0, 1)) / classes
    logit_grad = (prob_s * (coeff - row_dot[:, None]) / TEMP).astype(jnp.bfloat16)

    part = lax.dot_general(
        whole, logit_grad, (((1,), (1,)), ((), ())), preferred_element_type=jnp.float32
    )
    part = part.reshape(SIDE, SIDE, rows, tok_rows)
    part = jnp.where(core == 0, jnp.swapaxes(part, 0, 1), part)
    part = part.reshape(DP, CORES, rows // CORES, tok_rows)
    low, high = part[:, 0], part[:, 1]
    keep = jnp.where(core == 0, low, high)
    send = jnp.where(core == 0, high, low)
    keep = keep + lax.ppermute(send, "vocab", PAIR)
    share = lax.all_to_all(
        keep.astype(jnp.bfloat16), "vocab", 0, 0, tiled=True, axis_index_groups=COLUMN
    )
    hidden_grad = jnp.sum(share.astype(jnp.float32), 0).T.astype(jnp.bfloat16)
    return (logit_grad, hidden_grad)


def solution(mesh):
    return jax.shard_map(
        body,
        mesh=mesh,
        in_specs=(P("dp", None), P("dp", "vocab"), P("dp", "vocab")),
        out_specs=(P("dp", "vocab"), P("dp", "vocab")),
        check_vma=False,
    )
```

```python
import jax
import jax.numpy as jnp
from jax import lax
from jax.experimental import pallas as pl
from jax.experimental.pallas import tpu as pltpu
from jax.sharding import PartitionSpec as P

TEMP = 4
EPS = 1e-06
SIDE = 4
CHIPS = 16
CORES = 2
DP = SIDE * SIDE
VOCAB = CHIPS * CORES
AXES = ("dp", "vocab")
TILE = 128
GRANT = 22 * 1024 * 1024
F32, BF16 = jnp.float32, jnp.bfloat16


def _plane_groups(flip):
    groups = []
    for z in range(CHIPS):
        for core in range(CORES):
            for other in range(SIDE):
                along_x = (core ^ flip) == 0
                groups.append(
                    [
                        ((i * SIDE + other) if along_x else (other * SIDE + i)) * VOCAB + z * CORES + core
                        for i in range(SIDE)
                    ]
                )
    return groups


FIRST, SECOND = _plane_groups(0), _plane_groups(1)
COLUMN = [[z * CORES + core for z in range(CHIPS)] for core in range(CORES)]
PAIR = [(i, i ^ 1) for i in range(VOCAB)]


def spread(block, count, axis, groups=None):
    copies = jnp.broadcast_to(block[None], (count,) + block.shape)
    return lax.all_to_all(copies, axis, 0, 0, tiled=True, axis_index_groups=groups)


def _chunks(total, size):
    return [(at, min(at + size, total)) for at in range(0, total, size)]


def _rows(i, size):
    return pl.ds(pl.multiple_of(i * size, size), size)


def _loop(count, step, unroll):
    lax.fori_loop(0, count, lambda i, c: (step(i), c)[1], 0, unroll=unroll)


def _place(lane, *values):
    out = jnp.zeros(lane.shape, F32)
    for k, v in enumerate(values):
        out = jnp.where(lane == k, v, out)
    return out


def teacher_kernel(t_ref, e_ref, stat_ref, cols):
    lane = lax.broadcasted_iota(jnp.int32, (16, TILE), 1)

    def step(i):
        rows = _rows(i, 16)
        x = t_ref[rows, :].astype(F32) * (1.0 / TEMP)
        peak = jnp.max(x, axis=1, keepdims=True)
        e = jnp.exp(x - peak)
        e_ref[rows, :] = e
        cols[rows, :] = _place(
            lane, peak, jnp.sum(e, axis=1, keepdims=True), jnp.sum(e * e, axis=1, keepdims=True)
        )

    _loop(TILE // 16, step, 2)
    stat_ref[...] = cols[...].T[:8]


def student_kernel(h_ref, w_ref, et_ref, tstat_ref, e_ref, stat_ref, cols):
    width = w_ref.shape[1]
    lane = lax.broadcasted_iota(jnp.int32, (8, TILE), 1)
    for lo, hi in _chunks(width, 640):
        e_ref[:, lo:hi] = jnp.dot(
            h_ref[...], w_ref[:, lo:hi], preferred_element_type=F32
        ) * (1.0 / TEMP)

    def step(i):
        rows = _rows(i, 8)
        x = e_ref[rows, :]
        peak = jnp.max(x, axis=1, keepdims=True)
        e = jnp.exp(x - peak)
        e_ref[rows, :] = e
        cols[rows, :] = _place(
            lane,
            peak,
            jnp.sum(e, axis=1, keepdims=True),
            jnp.sum(e * e, axis=1, keepdims=True),
            jnp.sum(e * et_ref[rows, :], axis=1, keepdims=True),
        )

    _loop(TILE // 8, step, 4)
    mine = cols[...].T
    other = tstat_ref[...]
    stat_ref[0:1] = mine[0:1]
    stat_ref[1:2] = other[0:1]
    stat_ref[2:3] = mine[1:2]
    stat_ref[3:4] = other[1:2]
    stat_ref[4:5] = mine[2:3]
    stat_ref[5:6] = other[2:3]
    stat_ref[6:7] = mine[3:4]
    stat_ref[7:8] = jnp.zeros((1, TILE), F32)


def column_kernel(classes, es_ref, et_ref, own_ref, all_ref, sums_ref, terms_ref, acc, side):
    at = pl.program_id(0)
    parts = [all_ref[:, k, :] for k in range(7)]
    peak_s = jnp.max(parts[0], axis=0, keepdims=True)
    peak_t = jnp.max(parts[1], axis=0, keepdims=True)
    ws, wt = jnp.exp(parts[0] - peak_s), jnp.exp(parts[1] - peak_t)
    norm_s = jnp.sum(parts[2] * ws, axis=0, keepdims=True)
    norm_t = jnp.sum(parts[3] * wt, axis=0, keepdims=True)
    square_s = jnp.sum(parts[4] * (ws * ws), axis=0, keepdims=True)
    square_t = jnp.sum(parts[5] * (wt * wt), axis=0, keepdims=True)
    cross = jnp.sum(parts[6] * (ws * wt), axis=0, keepdims=True)
    row_var = classes * square_s / (norm_s * norm_s) - 1.0
    row_var_t = classes * square_t / (norm_t * norm_t) - 1.0
    row_den = jnp.sqrt((row_var + EPS) * (row_var_t + EPS))
    row_rho = (classes * cross / (norm_s * norm_t) - 1.0) / row_den
    side[0:1] = classes * jnp.exp(own_ref[0:1] - peak_s) / norm_s
    side[1:2] = classes * jnp.exp(own_ref[1:2] - peak_t) / norm_t
    side[2:3] = 1.0 / row_den
    side[3:4] = row_rho / (row_var + EPS)
    side[4:] = jnp.zeros((TILE - 4, TILE), F32)
    terms_ref[...] = side[...].T

    @pl.when(at == 0)
    def _():
        acc[...] = jnp.zeros_like(acc)

    for lo, hi in _chunks(es_ref.shape[1], 640):

        def step(i, carry, lo=lo, hi=hi):
            rows = _rows(i, 8)
            qs = es_ref[rows, lo:hi] * terms_ref[rows, 0:1]
            qt = et_ref[rows, lo:hi] * terms_ref[rows, 1:2]
            s, t, ss, tt, st = carry
            return (s + qs, t + qt, ss + qs * qs, tt + qt * qt, st + qs * qt)

        carry = tuple(acc[k, :, lo:hi] for k in range(5))
        carry = lax.fori_loop(0, TILE // 8, step, carry, unroll=4)
        for k in range(5):
            acc[k, :, lo:hi] = carry[k]

    @pl.when(at == pl.num_programs(0) - 1)
    def _():
        for k in range(5):
            total = jnp.sum(acc[k], axis=0, keepdims=True)
            for copy in range(SIDE):
                sums_ref[copy, k : k + 1, :] = total


def coefficient_kernel(
    tokens, es_ref, et_ref, terms_ref, sums_ref, g_ref, dots_ref, lines_ref, copies_ref, coef
):
    lane = lax.broadcasted_iota(jnp.int32, (8, TILE), 1)

    @pl.when(pl.program_id(0) == 0)
    def _():
        sums = [jnp.sum(sums_ref[:, k, :], axis=0, keepdims=True) / tokens for k in range(5)]
        mean_s, mean_t = sums[0], sums[1]
        var_s = sums[2] - mean_s * mean_s
        var_t = sums[3] - mean_t * mean_t
        den = jnp.sqrt((var_s + EPS) * (var_t + EPS))
        rho = (sums[4] - mean_s * mean_t) / den
        for k, v in enumerate((mean_s, mean_t, 1.0 / den, rho / (var_s + EPS))):
            coef[k] = jnp.broadcast_to(v, coef.shape[1:])

    def step(i):
        rows = _rows(i, 8)
        qs = es_ref[rows, :] * terms_ref[rows, 0:1]
        qt = et_ref[rows, :] * terms_ref[rows, 1:2]
        inner = qt * terms_ref[rows, 2:3] - qs * terms_ref[rows, 3:4]
        inner = inner + (qt - coef[1]) * coef[2] - (qs - coef[0]) * coef[3]
        g = -TEMP * inner
        g_ref[rows, :] = g
        dot = jnp.sum(qs * g, axis=1, keepdims=True)
        mass = jnp.sum(qs, axis=1, keepdims=True)
        dots_ref[rows, :] = _place(lane, dot, dot / jnp.maximum(mass, 1e-30))

    _loop(TILE // 8, step, 4)
    lines_ref[...] = dots_ref[...].T[:8]
    copies_ref[...] = jnp.broadcast_to(lines_ref[0:1].reshape(1, 1, TILE), copies_ref.shape)


def product_kernel(place_ref, es_ref, g_ref, terms_ref, dots_ref, w_ref, out_ref, left, res):
    def step(i):
        rows = _rows(i, 16)
        qs = es_ref[rows, :] * terms_ref[rows, 0:1]
        left[rows, :] = (qs * (g_ref[rows, :] - dots_ref[rows, 1:2]) * (1.0 / TEMP)).astype(BF16)
        left[pl.ds(pl.multiple_of(TILE + i * 16, 16), 16), :] = (qs * (1.0 / TEMP)).astype(BF16)

    _loop(TILE // 16, step, 2)
    res[...] = lax.dot_general(
        w_ref[...], left[...], (((1,), (1,)), ((), ())), preferred_element_type=F32
    )
    half = out_ref.shape[3]
    for j in range(DP):
        for core in range(CORES):
            lo = (j * CORES + core) * half
            away = (place_ref[DP] + core) % CORES
            for k in range(2):
                out_ref[k, away, place_ref[j]] = res[lo : lo + half, k * TILE : (k + 1) * TILE]


def pair_kernel(own_ref, other_ref, out_ref):
    a = [own_ref[k : k + 1] for k in range(7)]
    b = [other_ref[k : k + 1] for k in range(7)]
    peak_s, peak_t = jnp.maximum(a[0], b[0]), jnp.maximum(a[1], b[1])
    as_, bs = jnp.exp(a[0] - peak_s), jnp.exp(b[0] - peak_s)
    at, bt = jnp.exp(a[1] - peak_t), jnp.exp(b[1] - peak_t)
    both = (
        peak_s,
        peak_t,
        a[2] * as_ + b[2] * bs,
        a[3] * at + b[3] * bt,
        a[4] * (as_ * as_) + b[4] * (bs * bs),
        a[5] * (at * at) + b[5] * (bt * bt),
        a[6] * (as_ * at) + b[6] * (bs * bt),
        jnp.zeros_like(peak_s),
    )
    for k, v in enumerate(both):
        out_ref[:, k, :] = jnp.broadcast_to(v, (out_ref.shape[0], v.shape[1]))


def middle_kernel(parts_ref, out_ref):
    total = jnp.sum(parts_ref[...], axis=0)
    for k in range(out_ref.shape[0]):
        out_ref[k] = total


def shift_kernel(classes, products_ref, lines_ref, shares_ref, keep_ref, send_ref):
    total = jnp.sum(shares_ref[:, 0, :], axis=0, keepdims=True) / classes
    shift = lines_ref[1:2] - total
    for j in range(keep_ref.shape[0]):
        keep_ref[j] = products_ref[0, 0, j] + shift * products_ref[1, 0, j]
        send_ref[j] = products_ref[0, 1, j] + shift * products_ref[1, 1, j]


def add_kernel(a_ref, b_ref, out_ref):
    for j in range(out_ref.shape[0]):
        out_ref[j] = (a_ref[j] + b_ref[j]).astype(BF16)


def last_kernel(share_ref, out_ref):
    total = share_ref[0].astype(F32)
    for j in range(1, share_ref.shape[0]):
        total = total + share_ref[j].astype(F32)
    out_ref[...] = total


def gradient_kernel(classes, es_ref, g_ref, terms_ref, dots_ref, out_ref, side):
    total = jnp.sum(dots_ref[:, 0, :], axis=0, keepdims=True) / classes
    side[...] = jnp.broadcast_to(total, (TILE, TILE)).T

    def step(i):
        rows = _rows(i, 16)
        qs = es_ref[rows, :] * terms_ref[rows, 0:1]
        out_ref[rows, :] = (qs * (g_ref[rows, :] - side[rows, 0:1]) * (1.0 / TEMP)).astype(BF16)

    _loop(TILE // 16, step, 2)


def _call(kernel, steps, in_specs, out_specs, out_shape, scratch, flops, nbytes):
    return pl.pallas_call(
        kernel,
        grid=(steps,),
        in_specs=in_specs,
        out_specs=out_specs,
        out_shape=out_shape,
        scratch_shapes=scratch,
        compiler_params=pltpu.CompilerParams(
            dimension_semantics=("arbitrary",), vmem_limit_bytes=GRANT
        ),
        cost_estimate=pl.CostEstimate(flops=flops, bytes_accessed=nbytes, transcendentals=0),
    )


def _small(kernel, out_shape, *args):
    return pl.pallas_call(
        kernel,
        out_shape=out_shape,
        compiler_params=pltpu.CompilerParams(vmem_limit_bytes=GRANT),
        cost_estimate=pl.CostEstimate(flops=1000000, bytes_accessed=4000000, transcendentals=0),
    )(*args)


def body(student_hidden, head_weight, teacher_logits):
    tok, width = student_hidden.shape
    rows, cols = head_weight.shape
    classes = cols * VOCAB
    tokens = tok * DP
    steps = tok // TILE
    half = rows // CORES
    core = lax.axis_index("vocab") % CORES

    tile = pl.BlockSpec((TILE, cols), lambda i: (i, 0))
    strip = pl.BlockSpec((8, TILE), lambda i: (0, i))
    side = pl.BlockSpec((TILE, TILE), lambda i: (i, 0))
    whole_w = pl.BlockSpec((width, cols), lambda i: (0, 0), pipeline_mode=pl.Buffered(1))
    full = jax.ShapeDtypeStruct((tok, cols), F32)
    flat = jax.ShapeDtypeStruct((8, tok), F32)
    tall = jax.ShapeDtypeStruct((tok, TILE), F32)
    small = pltpu.VMEM((TILE, TILE), F32)
    area = tok * cols

    line = spread(head_weight, SIDE, AXES, FIRST).reshape(SIDE * rows, cols)
    whole = spread(line, SIDE, AXES, SECOND).reshape(width, cols)
    hid = student_hidden.reshape(tok, SIDE, SIDE, rows)
    hid = jnp.where(core == 0, jnp.swapaxes(hid, 1, 2), hid).reshape(tok, width)

    exp_t, stat_t = _call(
        teacher_kernel, steps, [tile], [tile, strip], [full, flat], [small], 8 * area, 6 * area
    )(teacher_logits)
    exp_s, stats = _call(
        student_kernel,
        steps,
        [pl.BlockSpec((TILE, width), lambda i: (i, 0)), whole_w, tile, strip],
        [tile, strip],
        [full, flat],
        [small],
        2 * area * width,
        8 * area,
    )(hid, whole, exp_t, stat_t)

    pair = _small(
        pair_kernel,
        jax.ShapeDtypeStruct((CHIPS, 8, tok), F32),
        stats,
        lax.ppermute(stats, "vocab", PAIR),
    )
    everyone = lax.all_to_all(pair, "vocab", 0, 0, tiled=True, axis_index_groups=COLUMN)
    sums, terms = _call(
        lambda *refs: column_kernel(classes, *refs),
        steps,
        [tile, tile, strip, pl.BlockSpec((CHIPS, 8, TILE), lambda i: (0, 0, i))],
        [pl.BlockSpec((SIDE, 5, cols), lambda i: (0, 0, 0)), side],
        [jax.ShapeDtypeStruct((SIDE, 5, cols), F32), tall],
        [pltpu.VMEM((5, 8, cols), F32), small],
        10 * area,
        8 * area,
    )(exp_s, exp_t, stats, everyone)

    sums = lax.all_to_all(sums, AXES, 0, 0, tiled=True, axis_index_groups=FIRST)
    sums = _small(middle_kernel, jax.ShapeDtypeStruct(sums.shape, F32), sums)
    sums = lax.all_to_all(sums, AXES, 0, 0, tiled=True, axis_index_groups=SECOND)
    coeff, dots, lines, copies = _call(
        lambda *refs: coefficient_kernel(tokens, *refs),
        steps,
        [tile, tile, side, pl.BlockSpec((SIDE, 5, cols), lambda i: (0, 0, 0))],
        [tile, side, strip, pl.BlockSpec((VOCAB, 1, TILE), lambda i: (0, 0, i))],
        [full, tall, flat, jax.ShapeDtypeStruct((VOCAB, 1, tok), F32)],
        [pltpu.VMEM((4, 8, cols), F32)],
        14 * area,
        12 * area,
    )(exp_s, exp_t, terms, sums)

    shares = lax.all_to_all(copies, "vocab", 0, 0, tiled=True)
    slot = jnp.arange(DP, dtype=jnp.int32)
    slot = jnp.where(core == 0, (slot % SIDE) * SIDE + slot // SIDE, slot)
    slot = jnp.concatenate([slot, core.astype(jnp.int32)[None]])
    products = _call(
        product_kernel,
        steps,
        [pl.BlockSpec(memory_space=pltpu.SMEM), tile, tile, side, side, whole_w],
        pl.BlockSpec((2, CORES, DP, half, TILE), lambda i: (0, 0, 0, 0, i)),
        jax.ShapeDtypeStruct((2, CORES, DP, half, tok), F32),
        [pltpu.VMEM((2 * TILE, cols), BF16), pltpu.VMEM((width, 2 * TILE), F32)],
        4 * area * width,
        16 * area,
    )(slot, exp_s, coeff, terms, dots, whole)
    piece = jax.ShapeDtypeStruct((DP, half, tok), F32)
    keep, send = _small(
        lambda *refs: shift_kernel(classes, *refs), [piece, piece], products, lines, shares
    )
    share = _small(
        add_kernel,
        jax.ShapeDtypeStruct((DP, half, tok), BF16),
        keep,
        lax.ppermute(send, "vocab", PAIR),
    )
    share = lax.all_to_all(share, "vocab", 0, 0, tiled=True, axis_index_groups=COLUMN)
    logit_grad = _call(
        lambda *refs: gradient_kernel(classes, *refs),
        steps,
        [tile, tile, side, pl.BlockSpec((VOCAB, 1, TILE), lambda i: (0, 0, i))],
        tile,
        jax.ShapeDtypeStruct((tok, cols), BF16),
        [small],
        4 * area,
        10 * area,
    )(exp_s, coeff, terms, shares)
    hidden_grad = _small(last_kernel, jax.ShapeDtypeStruct((half, tok), F32), share)
    return (logit_grad, hidden_grad.T.astype(BF16))


def solution(mesh):
    return jax.shard_map(
        body,
        mesh=mesh,
        in_specs=(P("dp", None), P("dp", "vocab"), P("dp", "vocab")),
        out_specs=(P("dp", "vocab"), P("dp", "vocab")),
        check_vma=False,
    )
```

```python
import jax
import jax.numpy as jnp
from jax import lax
from jax.experimental import pallas as pl
from jax.experimental.pallas import tpu as pltpu
from jax.sharding import PartitionSpec as P

TEMP = 4
EPS = 1e-06
SIDE = 4
CHIPS = 16
CORES = 2
DP = SIDE * SIDE
VOCAB = CHIPS * CORES
AXES = ("dp", "vocab")
TILE = 128
GRANT = 22 * 1024 * 1024
F32, BF16 = jnp.float32, jnp.bfloat16


def _plane_groups(flip):
    groups = []
    for z in range(CHIPS):
        for core in range(CORES):
            for other in range(SIDE):
                along_x = (core ^ flip) == 0
                groups.append(
                    [
                        ((i * SIDE + other) if along_x else (other * SIDE + i)) * VOCAB + z * CORES + core
                        for i in range(SIDE)
                    ]
                )
    return groups


FIRST, SECOND = _plane_groups(0), _plane_groups(1)
def _step_pairs(step):
    pairs = []
    for x in range(SIDE):
        for y in range(SIDE):
            for v in range(VOCAB):
                tx, ty = (x, (y + step) % SIDE) if v % CORES == 0 else ((x + step) % SIDE, y)
                pairs.append(((x * SIDE + y) * VOCAB + v, (tx * SIDE + ty) * VOCAB + v))
    return pairs


AHEAD, BACK = _step_pairs(1), _step_pairs(SIDE - 1)
COLUMN = [[z * CORES + core for z in range(CHIPS)] for core in range(CORES)]
PAIR = [(i, i ^ 1) for i in range(VOCAB)]


def spread(block, count, axis, groups=None):
    copies = jnp.broadcast_to(block[None], (count,) + block.shape)
    return lax.all_to_all(copies, axis, 0, 0, tiled=True, axis_index_groups=groups)


def _chunks(total, size):
    return [(at, min(at + size, total)) for at in range(0, total, size)]


def _rows(i, size):
    return pl.ds(pl.multiple_of(i * size, size), size)


def _loop(count, step, unroll):
    lax.fori_loop(0, count, lambda i, c: (step(i), c)[1], 0, unroll=unroll)


def product_kernel(place_ref, q_ref, g_ref, mean_ref, near_ref, far_ref, out_ref, left, res):
    def step(i):
        rows = _rows(i, 16)
        qs = q_ref[rows, :]
        left[rows, :] = (qs * (g_ref[rows, :] - mean_ref[rows, :]) * (1.0 / TEMP)).astype(BF16)
        left[pl.ds(pl.multiple_of(TILE + i * 16, 16), 16), :] = (qs * (1.0 / TEMP)).astype(BF16)

    _loop(TILE // 16, step, 2)
    cut = near_ref.shape[0]
    for part_ref, lo, hi in ((near_ref, 0, cut), (far_ref, cut, res.shape[0])):
        res[lo:hi] = lax.dot_general(
            part_ref[...], left[...], (((1,), (1,)), ((), ())), preferred_element_type=F32
        )
    half = out_ref.shape[3]
    for j in range(DP):
        for core in range(CORES):
            lo = (j * CORES + core) * half
            away = (place_ref[DP] + core) % CORES
            for k in range(2):
                out_ref[k, away, place_ref[j]] = res[lo : lo + half, k * TILE : (k + 1) * TILE]


def shift_kernel(classes, mean_ref, shares_ref, products_ref, keep_ref, send_ref):
    shift = mean_ref[...] - jnp.sum(shares_ref[:, 0, :], axis=0, keepdims=True) / classes
    for j in range(keep_ref.shape[0]):
        keep_ref[j] = products_ref[0, 0, j] + shift * products_ref[1, 0, j]
        send_ref[j] = products_ref[0, 1, j] + shift * products_ref[1, 1, j]


def add_kernel(a_ref, b_ref, out_ref):
    for j in range(out_ref.shape[0]):
        out_ref[j] = (a_ref[j] + b_ref[j]).astype(BF16)


def last_kernel(share_ref, out_ref):
    total = share_ref[0].astype(F32)
    for j in range(1, share_ref.shape[0]):
        total = total + share_ref[j].astype(F32)
    out_ref[...] = total


def _call(kernel, steps, in_specs, out_specs, out_shape, scratch, flops, nbytes):
    return pl.pallas_call(
        kernel,
        grid=(steps,),
        in_specs=in_specs,
        out_specs=out_specs,
        out_shape=out_shape,
        scratch_shapes=scratch,
        compiler_params=pltpu.CompilerParams(
            dimension_semantics=("arbitrary",), vmem_limit_bytes=GRANT
        ),
        cost_estimate=pl.CostEstimate(flops=flops, bytes_accessed=nbytes, transcendentals=0),
    )


def _far(x):
    return pltpu.with_memory_space_constraint(x, pltpu.HBM)


def _small(kernel, out_shape, *args):
    return pl.pallas_call(
        kernel,
        out_shape=out_shape,
        compiler_params=pltpu.CompilerParams(vmem_limit_bytes=GRANT),
        cost_estimate=pl.CostEstimate(flops=1000000, bytes_accessed=4000000, transcendentals=0),
    )(*args)


def merge(parts):
    peak_s, peak_t = jnp.max(parts[:, 0], 0), jnp.max(parts[:, 1], 0)
    ws, wt = jnp.exp(parts[:, 0] - peak_s), jnp.exp(parts[:, 1] - peak_t)
    return jnp.stack(
        [
            peak_s,
            peak_t,
            jnp.sum(parts[:, 2] * ws, 0),
            jnp.sum(parts[:, 3] * wt, 0),
            jnp.sum(parts[:, 4] * (ws * ws), 0),
            jnp.sum(parts[:, 5] * (wt * wt), 0),
            jnp.sum(parts[:, 6] * (ws * wt), 0),
        ]
    )


def body(student_hidden, head_weight, teacher_logits):
    tok_rows, width = student_hidden.shape
    rows, vocab_cols = head_weight.shape
    classes = vocab_cols * VOCAB
    tokens = tok_rows * DP
    core = lax.axis_index("vocab") % CORES

    line = spread(head_weight, SIDE, AXES, FIRST).reshape(SIDE * rows, vocab_cols)
    mine = lax.axis_index("dp")
    place = jnp.where(core == 0, mine % SIDE, mine // SIDE)
    offsets = (0, SIDE - 1, 1, 2)
    hid = student_hidden.reshape(tok_rows, SIDE, SIDE, rows)
    hid = jnp.where(core == 0, jnp.swapaxes(hid, 1, 2), hid).reshape(tok_rows, SIDE, SIDE * rows)
    hid = [
        lax.dynamic_slice_in_dim(hid, (place + o) % SIDE, 1, 1).reshape(tok_rows, SIDE * rows)
        for o in offsets
    ]
    line, hid_near, hid_far = lax.optimization_barrier(
        (line, jnp.concatenate(hid[:3], 1), hid[3])
    )
    top, low_half = line[: SIDE * rows // 2], line[SIDE * rows // 2 :]
    left_top = lax.ppermute(top, AXES, AHEAD)
    right_low = lax.ppermute(low_half, AXES, BACK)
    left_low = lax.ppermute(low_half, AXES, AHEAD)
    right_top = lax.ppermute(top, AXES, BACK)
    far = jnp.concatenate(
        [lax.ppermute(left_top, AXES, AHEAD), lax.ppermute(right_low, AXES, BACK)], 0
    )
    near = jnp.concatenate([line, left_top, left_low, right_top, right_low], 0)

    logits = jnp.dot(hid_near, near, preferred_element_type=F32)
    logits = logits + jnp.dot(hid_far, far, preferred_element_type=F32)
    scaled_student = logits / TEMP
    scaled_teacher = teacher_logits.astype(jnp.float32) / TEMP
    own_s = jnp.max(scaled_student, axis=1)
    own_t = jnp.max(scaled_teacher, axis=1)
    exp_s = jnp.exp(scaled_student - own_s[:, None])
    exp_t = jnp.exp(scaled_teacher - own_t[:, None])
    stats = jnp.stack(
        [
            own_s,
            own_t,
            jnp.sum(exp_s, 1),
            jnp.sum(exp_t, 1),
            jnp.sum(exp_s * exp_s, 1),
            jnp.sum(exp_t * exp_t, 1),
            jnp.sum(exp_s * exp_t, 1),
        ]
    )
    stats = merge(jnp.stack([stats, lax.ppermute(stats, "vocab", PAIR)]))
    stats = merge(spread(stats, CHIPS, "vocab", COLUMN))
    norm_s, norm_t = stats[2], stats[3]
    row_var = classes * stats[4] / (norm_s * norm_s) - 1.0
    row_var_t = classes * stats[5] / (norm_t * norm_t) - 1.0
    cross = classes * stats[6] / (norm_s * norm_t) - 1.0
    row_den = jnp.sqrt((row_var + EPS) * (row_var_t + EPS))
    row_rho = cross / row_den
    prob_s = exp_s * (classes * jnp.exp(own_s - stats[0]) / norm_s)[:, None]
    prob_t = exp_t * (classes * jnp.exp(own_t - stats[1]) / norm_t)[:, None]

    sums = jnp.stack(
        [
            jnp.sum(prob_s, 0),
            jnp.sum(prob_t, 0),
            jnp.sum(prob_s * prob_s, 0),
            jnp.sum(prob_t * prob_t, 0),
            jnp.sum(prob_s * prob_t, 0),
        ]
    )
    sums = jnp.sum(spread(sums, SIDE, AXES, FIRST), 0)
    sums = jnp.sum(spread(sums, SIDE, AXES, SECOND), 0)
    mean_s = sums[0] / tokens
    mean_t = sums[1] / tokens
    col_var = sums[2] / tokens - mean_s * mean_s
    col_var_t = sums[3] / tokens - mean_t * mean_t
    col_cov = sums[4] / tokens - mean_s * mean_t
    col_den = jnp.sqrt((col_var + EPS) * (col_var_t + EPS))
    col_rho = col_cov / col_den

    inner = prob_t / row_den[:, None] - (row_rho / (row_var + EPS))[:, None] * prob_s
    inner = inner + (prob_t - mean_t[None, :]) / col_den[None, :]
    inner = inner - (col_rho / (col_var + EPS))[None, :] * (prob_s - mean_s[None, :])
    coeff = -TEMP * inner
    steps = tok_rows // TILE
    half = rows // CORES
    area = tok_rows * vocab_cols
    own_dot = jnp.sum(prob_s * coeff, 1)
    mean = own_dot / jnp.maximum(jnp.sum(prob_s, 1), 1e-30)
    shares = spread(own_dot[None], VOCAB, "vocab")
    turn = jnp.repeat((place + jnp.array(offsets, jnp.int32)) % SIDE, SIDE)
    along = jnp.tile(jnp.arange(SIDE, dtype=jnp.int32), SIDE)
    slot = jnp.where(core == 0, along * SIDE + turn, turn * SIDE + along)
    slot = jnp.concatenate([slot, core.astype(jnp.int32)[None]])
    tile = pl.BlockSpec((TILE, vocab_cols), lambda i: (i, 0))
    products = _call(
        product_kernel,
        steps,
        [
            pl.BlockSpec(memory_space=pltpu.SMEM),
            tile,
            tile,
            pl.BlockSpec((TILE, 1), lambda i: (i, 0)),
            pl.BlockSpec(near.shape, lambda i: (0, 0), pipeline_mode=pl.Buffered(1)),
            pl.BlockSpec(far.shape, lambda i: (0, 0), pipeline_mode=pl.Buffered(1)),
        ],
        pl.BlockSpec((2, CORES, DP, half, TILE), lambda i: (0, 0, 0, 0, i)),
        jax.ShapeDtypeStruct((2, CORES, DP, half, tok_rows), F32),
        [pltpu.VMEM((2 * TILE, vocab_cols), BF16), pltpu.VMEM((width, 2 * TILE), F32)],
        4 * area * width,
        16 * area,
    )(slot, _far(prob_s), _far(coeff), mean[:, None], _far(near), _far(far))
    row_dot = jnp.sum(shares, (0, 1)) / classes
    piece = jax.ShapeDtypeStruct((DP, half, tok_rows), F32)
    keep, send = _small(
        lambda *refs: shift_kernel(classes, *refs), [piece, piece], mean[None], shares, products
    )
    share = _small(
        add_kernel,
        jax.ShapeDtypeStruct((DP, half, tok_rows), BF16),
        keep,
        lax.ppermute(send, "vocab", PAIR),
    )
    share = lax.all_to_all(share, "vocab", 0, 0, tiled=True, axis_index_groups=COLUMN)
    logit_grad = (prob_s * (coeff - row_dot[:, None]) / TEMP).astype(BF16)
    hidden_grad = _small(last_kernel, jax.ShapeDtypeStruct((half, tok_rows), F32), share)
    return (logit_grad, hidden_grad.T.astype(BF16))


def solution(mesh):
    return jax.shard_map(
        body,
        mesh=mesh,
        in_specs=(P("dp", None), P("dp", "vocab"), P("dp", "vocab")),
        out_specs=(P("dp", "vocab"), P("dp", "vocab")),
        check_vma=False,
    )
```

```python
import jax
import jax.numpy as jnp
from jax import lax
from jax.experimental import pallas as pl
from jax.experimental.pallas import tpu as pltpu
from jax.sharding import PartitionSpec as P

TEMP = 4
EPS = 1e-06
SIDE = 4
CHIPS = 16
CORES = 2
DP = SIDE * SIDE
VOCAB = CHIPS * CORES
AXES = ("dp", "vocab")
TILE = 128
GRANT = 22 * 1024 * 1024
F32, BF16 = jnp.float32, jnp.bfloat16


def _plane_groups(flip):
    groups = []
    for z in range(CHIPS):
        for core in range(CORES):
            for other in range(SIDE):
                along_x = (core ^ flip) == 0
                groups.append(
                    [
                        ((i * SIDE + other) if along_x else (other * SIDE + i)) * VOCAB + z * CORES + core
                        for i in range(SIDE)
                    ]
                )
    return groups


FIRST, SECOND = _plane_groups(0), _plane_groups(1)
def _step_pairs(step, second):
    pairs = []
    for x in range(SIDE):
        for y in range(SIDE):
            for v in range(VOCAB):
                along_x = (v % CORES == 0) != second
                tx, ty = ((x + step) % SIDE, y) if along_x else (x, (y + step) % SIDE)
                pairs.append(((x * SIDE + y) * VOCAB + v, (tx * SIDE + ty) * VOCAB + v))
    return pairs


OVER = [_step_pairs(step, False) for step in (1, SIDE - 1, 2)]
AHEAD, BACK = _step_pairs(1, True), _step_pairs(SIDE - 1, True)
COLUMN = [[z * CORES + core for z in range(CHIPS)] for core in range(CORES)]
PAIR = [(i, i ^ 1) for i in range(VOCAB)]


def spread(block, count, axis, groups=None):
    copies = jnp.broadcast_to(block[None], (count,) + block.shape)
    return lax.all_to_all(copies, axis, 0, 0, tiled=True, axis_index_groups=groups)


def _chunks(total, size):
    return [(at, min(at + size, total)) for at in range(0, total, size)]


def _rows(i, size):
    return pl.ds(pl.multiple_of(i * size, size), size)


def _loop(count, step, unroll):
    lax.fori_loop(0, count, lambda i, c: (step(i), c)[1], 0, unroll=unroll)


def product_kernel(place_ref, q_ref, g_ref, mean_ref, near_ref, far_ref, out_ref, left, res):
    def step(i):
        rows = _rows(i, 16)
        qs = q_ref[rows, :]
        left[rows, :] = (qs * (g_ref[rows, :] - mean_ref[rows, :]) * (1.0 / TEMP)).astype(BF16)
        left[pl.ds(pl.multiple_of(TILE + i * 16, 16), 16), :] = (qs * (1.0 / TEMP)).astype(BF16)

    _loop(TILE // 16, step, 2)
    cut = near_ref.shape[0]
    for part_ref, lo, hi in ((near_ref, 0, cut), (far_ref, cut, res.shape[0])):
        res[lo:hi] = lax.dot_general(
            part_ref[...], left[...], (((1,), (1,)), ((), ())), preferred_element_type=F32
        )
    half = out_ref.shape[3]
    for j in range(DP):
        for core in range(CORES):
            lo = (j * CORES + core) * half
            away = (place_ref[DP] + core) % CORES
            for k in range(2):
                out_ref[k, away, place_ref[j]] = res[lo : lo + half, k * TILE : (k + 1) * TILE]


def shift_kernel(classes, mean_ref, shares_ref, products_ref, keep_ref, send_ref):
    shift = mean_ref[...] - jnp.sum(shares_ref[:, 0, :], axis=0, keepdims=True) / classes
    for j in range(keep_ref.shape[0]):
        keep_ref[j] = products_ref[0, 0, j] + shift * products_ref[1, 0, j]
        send_ref[j] = products_ref[0, 1, j] + shift * products_ref[1, 1, j]


def add_kernel(a_ref, b_ref, out_ref):
    for j in range(out_ref.shape[0]):
        out_ref[j] = (a_ref[j] + b_ref[j]).astype(BF16)


def last_kernel(share_ref, out_ref):
    total = share_ref[0].astype(F32)
    for j in range(1, share_ref.shape[0]):
        total = total + share_ref[j].astype(F32)
    out_ref[...] = total


def _call(kernel, steps, in_specs, out_specs, out_shape, scratch, flops, nbytes):
    return pl.pallas_call(
        kernel,
        grid=(steps,),
        in_specs=in_specs,
        out_specs=out_specs,
        out_shape=out_shape,
        scratch_shapes=scratch,
        compiler_params=pltpu.CompilerParams(
            dimension_semantics=("arbitrary",), vmem_limit_bytes=GRANT
        ),
        cost_estimate=pl.CostEstimate(flops=flops, bytes_accessed=nbytes, transcendentals=0),
    )


def _far(x):
    return pltpu.with_memory_space_constraint(x, pltpu.HBM)


def _small(kernel, out_shape, *args):
    return pl.pallas_call(
        kernel,
        out_shape=out_shape,
        compiler_params=pltpu.CompilerParams(vmem_limit_bytes=GRANT),
        cost_estimate=pl.CostEstimate(flops=1000000, bytes_accessed=4000000, transcendentals=0),
    )(*args)


def merge(parts):
    peak_s, peak_t = jnp.max(parts[:, 0], 0), jnp.max(parts[:, 1], 0)
    ws, wt = jnp.exp(parts[:, 0] - peak_s), jnp.exp(parts[:, 1] - peak_t)
    return jnp.stack(
        [
            peak_s,
            peak_t,
            jnp.sum(parts[:, 2] * ws, 0),
            jnp.sum(parts[:, 3] * wt, 0),
            jnp.sum(parts[:, 4] * (ws * ws), 0),
            jnp.sum(parts[:, 5] * (wt * wt), 0),
            jnp.sum(parts[:, 6] * (ws * wt), 0),
        ]
    )


def body(student_hidden, head_weight, teacher_logits):
    tok_rows, width = student_hidden.shape
    rows, vocab_cols = head_weight.shape
    classes = vocab_cols * VOCAB
    tokens = tok_rows * DP
    core = lax.axis_index("vocab") % CORES

    behind, before, across = (lax.ppermute(head_weight, AXES, pairs) for pairs in OVER)

    mine = lax.axis_index("dp")
    down, right = mine // SIDE, mine % SIDE
    first = jnp.where(core == 0, down, right)
    second = jnp.where(core == 0, right, down)
    offsets = (0, SIDE - 1, 1, 2)
    hid = student_hidden.reshape(tok_rows, SIDE, SIDE, rows)
    hid = jnp.where(core == 0, jnp.swapaxes(hid, 1, 2), hid)
    hid = jnp.concatenate(
        [lax.dynamic_slice_in_dim(hid, (first + o) % SIDE, 1, 2) for o in offsets], 2
    ).reshape(tok_rows, SIDE, SIDE * rows)
    hid = [
        lax.dynamic_slice_in_dim(hid, (second + o) % SIDE, 1, 1).reshape(tok_rows, SIDE * rows)
        for o in offsets
    ]
    turn = jnp.stack([(second + offsets[k // SIDE]) % SIDE for k in range(DP)])
    along = jnp.stack([(first + offsets[k % SIDE]) % SIDE for k in range(DP)])
    slot = jnp.where(core == 0, along * SIDE + turn, turn * SIDE + along)
    slot = jnp.concatenate([slot, core[None]]).astype(jnp.int32)
    behind, hid_near, hid_far, slot = lax.optimization_barrier(
        (behind, jnp.concatenate(hid[:3], 1), hid[3], slot)
    )
    early = jnp.concatenate([head_weight, behind], 0)
    left_early = lax.ppermute(early, AXES, AHEAD)
    right_early = lax.ppermute(early, AXES, BACK)
    late = jnp.concatenate([before, across], 0)
    right_late = lax.ppermute(late, AXES, BACK)
    left_late = lax.ppermute(late, AXES, AHEAD)
    far = jnp.concatenate(
        [lax.ppermute(left_early, AXES, AHEAD), lax.ppermute(right_late, AXES, BACK)], 0
    )
    near = jnp.concatenate([early, late, left_early, left_late, right_early, right_late], 0)
    logits = jnp.dot(hid_near, near, preferred_element_type=F32)
    logits = logits + jnp.dot(hid_far, far, preferred_element_type=F32)
    scaled_student = logits / TEMP
    scaled_teacher = teacher_logits.astype(jnp.float32) / TEMP
    own_s = jnp.max(scaled_student, axis=1)
    own_t = jnp.max(scaled_teacher, axis=1)
    exp_s = jnp.exp(scaled_student - own_s[:, None])
    exp_t = jnp.exp(scaled_teacher - own_t[:, None])
    stats = jnp.stack(
        [
            own_s,
            own_t,
            jnp.sum(exp_s, 1),
            jnp.sum(exp_t, 1),
            jnp.sum(exp_s * exp_s, 1),
            jnp.sum(exp_t * exp_t, 1),
            jnp.sum(exp_s * exp_t, 1),
        ]
    )
    stats = merge(jnp.stack([stats, lax.ppermute(stats, "vocab", PAIR)]))
    stats = merge(spread(stats, CHIPS, "vocab", COLUMN))
    norm_s, norm_t = stats[2], stats[3]
    row_var = classes * stats[4] / (norm_s * norm_s) - 1.0
    row_var_t = classes * stats[5] / (norm_t * norm_t) - 1.0
    cross = classes * stats[6] / (norm_s * norm_t) - 1.0
    row_den = jnp.sqrt((row_var + EPS) * (row_var_t + EPS))
    row_rho = cross / row_den
    prob_s = exp_s * (classes * jnp.exp(own_s - stats[0]) / norm_s)[:, None]
    prob_t = exp_t * (classes * jnp.exp(own_t - stats[1]) / norm_t)[:, None]

    sums = jnp.stack(
        [
            jnp.sum(prob_s, 0),
            jnp.sum(prob_t, 0),
            jnp.sum(prob_s * prob_s, 0),
            jnp.sum(prob_t * prob_t, 0),
            jnp.sum(prob_s * prob_t, 0),
        ]
    )
    sums = jnp.sum(spread(sums, SIDE, AXES, FIRST), 0)
    sums = jnp.sum(spread(sums, SIDE, AXES, SECOND), 0)
    mean_s = sums[0] / tokens
    mean_t = sums[1] / tokens
    col_var = sums[2] / tokens - mean_s * mean_s
    col_var_t = sums[3] / tokens - mean_t * mean_t
    col_cov = sums[4] / tokens - mean_s * mean_t
    col_den = jnp.sqrt((col_var + EPS) * (col_var_t + EPS))
    col_rho = col_cov / col_den

    inner = prob_t / row_den[:, None] - (row_rho / (row_var + EPS))[:, None] * prob_s
    inner = inner + (prob_t - mean_t[None, :]) / col_den[None, :]
    inner = inner - (col_rho / (col_var + EPS))[None, :] * (prob_s - mean_s[None, :])
    coeff = -TEMP * inner
    steps = tok_rows // TILE
    half = rows // CORES
    area = tok_rows * vocab_cols
    own_dot = jnp.sum(prob_s * coeff, 1)
    mean = own_dot / jnp.maximum(jnp.sum(prob_s, 1), 1e-30)
    shares = spread(own_dot[None], VOCAB, "vocab")
    tile = pl.BlockSpec((TILE, vocab_cols), lambda i: (i, 0))
    products = _call(
        product_kernel,
        steps,
        [
            pl.BlockSpec(memory_space=pltpu.SMEM),
            tile,
            tile,
            pl.BlockSpec((TILE, 1), lambda i: (i, 0)),
            pl.BlockSpec(near.shape, lambda i: (0, 0), pipeline_mode=pl.Buffered(1)),
            pl.BlockSpec(far.shape, lambda i: (0, 0), pipeline_mode=pl.Buffered(1)),
        ],
        pl.BlockSpec((2, CORES, DP, half, TILE), lambda i: (0, 0, 0, 0, i)),
        jax.ShapeDtypeStruct((2, CORES, DP, half, tok_rows), F32),
        [pltpu.VMEM((2 * TILE, vocab_cols), BF16), pltpu.VMEM((width, 2 * TILE), F32)],
        4 * area * width,
        16 * area,
    )(slot, _far(prob_s), _far(coeff), mean[:, None], _far(near), _far(far))
    row_dot = jnp.sum(shares, (0, 1)) / classes
    piece = jax.ShapeDtypeStruct((DP, half, tok_rows), F32)
    keep, send = _small(
        lambda *refs: shift_kernel(classes, *refs), [piece, piece], mean[None], shares, products
    )
    share = _small(
        add_kernel,
        jax.ShapeDtypeStruct((DP, half, tok_rows), BF16),
        keep,
        lax.ppermute(send, "vocab", PAIR),
    )
    share = lax.all_to_all(share, "vocab", 0, 0, tiled=True, axis_index_groups=COLUMN)
    logit_grad = (prob_s * (coeff - row_dot[:, None]) / TEMP).astype(BF16)
    hidden_grad = _small(last_kernel, jax.ShapeDtypeStruct((half, tok_rows), F32), share)
    return (logit_grad, hidden_grad.T.astype(BF16))


def solution(mesh):
    return jax.shard_map(
        body,
        mesh=mesh,
        in_specs=(P("dp", None), P("dp", "vocab"), P("dp", "vocab")),
        out_specs=(P("dp", "vocab"), P("dp", "vocab")),
        check_vma=False,
    )
```

```python
import jax
import jax.numpy as jnp
from jax import lax
from jax.experimental import pallas as pl
from jax.experimental.pallas import tpu as pltpu
from jax.sharding import PartitionSpec as P

TEMP = 4
EPS = 1e-06
SIDE = 4
CHIPS = 16
CORES = 2
DP = SIDE * SIDE
VOCAB = CHIPS * CORES
AXES = ("dp", "vocab")
TILE = 128
GRANT = 22 * 1024 * 1024
F32, BF16 = jnp.float32, jnp.bfloat16


def _plane_groups(flip):
    groups = []
    for z in range(CHIPS):
        for core in range(CORES):
            for other in range(SIDE):
                along_x = (core ^ flip) == 0
                groups.append(
                    [
                        ((i * SIDE + other) if along_x else (other * SIDE + i)) * VOCAB + z * CORES + core
                        for i in range(SIDE)
                    ]
                )
    return groups


FIRST, SECOND = _plane_groups(0), _plane_groups(1)
def _step_pairs(step, second):
    pairs = []
    for x in range(SIDE):
        for y in range(SIDE):
            for v in range(VOCAB):
                along_x = (v % CORES == 0) != second
                tx, ty = ((x + step) % SIDE, y) if along_x else (x, (y + step) % SIDE)
                pairs.append(((x * SIDE + y) * VOCAB + v, (tx * SIDE + ty) * VOCAB + v))
    return pairs


OVER = [_step_pairs(step, False) for step in (1, SIDE - 1, 2)]
AHEAD, BACK = _step_pairs(1, True), _step_pairs(SIDE - 1, True)
COLUMN = [[z * CORES + core for z in range(CHIPS)] for core in range(CORES)]
PAIR = [(i, i ^ 1) for i in range(VOCAB)]


def spread(block, count, axis, groups=None):
    copies = jnp.broadcast_to(block[None], (count,) + block.shape)
    return lax.all_to_all(copies, axis, 0, 0, tiled=True, axis_index_groups=groups)


def _chunks(total, size):
    return [(at, min(at + size, total)) for at in range(0, total, size)]


def _rows(i, size):
    return pl.ds(pl.multiple_of(i * size, size), size)


def _loop(count, step, unroll):
    lax.fori_loop(0, count, lambda i, c: (step(i), c)[1], 0, unroll=unroll)


def product_kernel(place_ref, q_ref, g_ref, mean_ref, near_ref, far_ref, out_ref, left, res):
    def step(i):
        rows = _rows(i, 16)
        qs = q_ref[rows, :]
        left[rows, :] = (qs * (g_ref[rows, :] - mean_ref[rows, :]) * (1.0 / TEMP)).astype(BF16)
        left[pl.ds(pl.multiple_of(TILE + i * 16, 16), 16), :] = (qs * (1.0 / TEMP)).astype(BF16)

    _loop(TILE // 16, step, 2)
    cut = near_ref.shape[0]
    for part_ref, lo, hi in ((near_ref, 0, cut), (far_ref, cut, res.shape[0])):
        res[lo:hi] = lax.dot_general(
            part_ref[...], left[...], (((1,), (1,)), ((), ())), preferred_element_type=F32
        )
    half = out_ref.shape[3]
    for j in range(DP):
        for core in range(CORES):
            lo = (j * CORES + core) * half
            away = (place_ref[DP] + core) % CORES
            for k in range(2):
                out_ref[k, away, place_ref[j]] = res[lo : lo + half, k * TILE : (k + 1) * TILE]


def shift_kernel(classes, mean_ref, shares_ref, products_ref, keep_ref, send_ref):
    shift = mean_ref[...] - jnp.sum(shares_ref[:, 0, :], axis=0, keepdims=True) / classes
    for j in range(keep_ref.shape[0]):
        keep_ref[j] = products_ref[0, 0, j] + shift * products_ref[1, 0, j]
        send_ref[j] = products_ref[0, 1, j] + shift * products_ref[1, 1, j]


def add_kernel(a_ref, b_ref, out_ref, packed):
    half, tok = a_ref.shape[1:]
    for j in range(out_ref.shape[0]):
        for k in range(tok // TILE):
            at = slice(k * TILE, (k + 1) * TILE)
            packed[j, k * half : (k + 1) * half] = a_ref[j, :, at] + b_ref[j, :, at]
        out_ref[j] = packed[j].astype(BF16)


def last_kernel(share_ref, out_ref):
    half, tok = out_ref.shape
    total = share_ref[0].astype(F32)
    for j in range(1, share_ref.shape[0]):
        total = total + share_ref[j].astype(F32)
    for k in range(tok // TILE):
        out_ref[:, k * TILE : (k + 1) * TILE] = total[k * half : (k + 1) * half]


def _call(kernel, steps, in_specs, out_specs, out_shape, scratch, flops, nbytes):
    return pl.pallas_call(
        kernel,
        grid=(steps,),
        in_specs=in_specs,
        out_specs=out_specs,
        out_shape=out_shape,
        scratch_shapes=scratch,
        compiler_params=pltpu.CompilerParams(
            dimension_semantics=("arbitrary",), vmem_limit_bytes=GRANT
        ),
        cost_estimate=pl.CostEstimate(flops=flops, bytes_accessed=nbytes, transcendentals=0),
    )


def _far(x):
    return pltpu.with_memory_space_constraint(x, pltpu.HBM)


def _small(kernel, out_shape, *args, scratch=()):
    return pl.pallas_call(
        kernel,
        out_shape=out_shape,
        scratch_shapes=scratch,
        compiler_params=pltpu.CompilerParams(vmem_limit_bytes=GRANT),
        cost_estimate=pl.CostEstimate(flops=1000000, bytes_accessed=4000000, transcendentals=0),
    )(*args)


def merge(parts):
    peak_s, peak_t = jnp.max(parts[:, 0], 0), jnp.max(parts[:, 1], 0)
    ws, wt = jnp.exp(parts[:, 0] - peak_s), jnp.exp(parts[:, 1] - peak_t)
    return jnp.stack(
        [
            peak_s,
            peak_t,
            jnp.sum(parts[:, 2] * ws, 0),
            jnp.sum(parts[:, 3] * wt, 0),
            jnp.sum(parts[:, 4] * (ws * ws), 0),
            jnp.sum(parts[:, 5] * (wt * wt), 0),
            jnp.sum(parts[:, 6] * (ws * wt), 0),
        ]
    )


def body(student_hidden, head_weight, teacher_logits):
    tok_rows, width = student_hidden.shape
    rows, vocab_cols = head_weight.shape
    classes = vocab_cols * VOCAB
    tokens = tok_rows * DP
    core = lax.axis_index("vocab") % CORES

    behind, before, across = (lax.ppermute(head_weight, AXES, pairs) for pairs in OVER)

    mine = lax.axis_index("dp")
    down, right = mine // SIDE, mine % SIDE
    first = jnp.where(core == 0, down, right)
    second = jnp.where(core == 0, right, down)
    offsets = (0, SIDE - 1, 1, 2)
    hid = student_hidden.reshape(tok_rows, SIDE, SIDE, rows)
    hid = jnp.where(core == 0, jnp.swapaxes(hid, 1, 2), hid)
    hid = jnp.concatenate(
        [lax.dynamic_slice_in_dim(hid, (first + o) % SIDE, 1, 2) for o in offsets], 2
    ).reshape(tok_rows, SIDE, SIDE * rows)
    hid = [
        lax.dynamic_slice_in_dim(hid, (second + o) % SIDE, 1, 1).reshape(tok_rows, SIDE * rows)
        for o in offsets
    ]
    turn = jnp.stack([(second + offsets[k // SIDE]) % SIDE for k in range(DP)])
    along = jnp.stack([(first + offsets[k % SIDE]) % SIDE for k in range(DP)])
    slot = jnp.where(core == 0, along * SIDE + turn, turn * SIDE + along)
    slot = jnp.concatenate([slot, core[None]]).astype(jnp.int32)
    behind, hid_near, hid_far, slot = lax.optimization_barrier(
        (behind, jnp.concatenate(hid[:3], 1), hid[3], slot)
    )
    early = jnp.concatenate([head_weight, behind], 0)
    left_early = lax.ppermute(early, AXES, AHEAD)
    right_early = lax.ppermute(early, AXES, BACK)
    late = jnp.concatenate([before, across], 0)
    right_late = lax.ppermute(late, AXES, BACK)
    left_late = lax.ppermute(late, AXES, AHEAD)
    far = jnp.concatenate(
        [lax.ppermute(left_early, AXES, AHEAD), lax.ppermute(right_late, AXES, BACK)], 0
    )
    near = jnp.concatenate([early, late, left_early, left_late, right_early, right_late], 0)
    logits = jnp.dot(hid_near, near, preferred_element_type=F32)
    logits = logits + jnp.dot(hid_far, far, preferred_element_type=F32)
    scaled_student = logits / TEMP
    scaled_teacher = teacher_logits.astype(jnp.float32) / TEMP
    own_s = jnp.max(scaled_student, axis=1)
    own_t = jnp.max(scaled_teacher, axis=1)
    exp_s = jnp.exp(scaled_student - own_s[:, None])
    exp_t = jnp.exp(scaled_teacher - own_t[:, None])
    stats = jnp.stack(
        [
            own_s,
            own_t,
            jnp.sum(exp_s, 1),
            jnp.sum(exp_t, 1),
            jnp.sum(exp_s * exp_s, 1),
            jnp.sum(exp_t * exp_t, 1),
            jnp.sum(exp_s * exp_t, 1),
        ]
    )
    stats = merge(jnp.stack([stats, lax.ppermute(stats, "vocab", PAIR)]))
    stats = merge(spread(stats, CHIPS, "vocab", COLUMN))
    norm_s, norm_t = stats[2], stats[3]
    row_var = classes * stats[4] / (norm_s * norm_s) - 1.0
    row_var_t = classes * stats[5] / (norm_t * norm_t) - 1.0
    cross = classes * stats[6] / (norm_s * norm_t) - 1.0
    row_den = jnp.sqrt((row_var + EPS) * (row_var_t + EPS))
    row_rho = cross / row_den
    prob_s = exp_s * (classes * jnp.exp(own_s - stats[0]) / norm_s)[:, None]
    prob_t = exp_t * (classes * jnp.exp(own_t - stats[1]) / norm_t)[:, None]

    sums = jnp.stack(
        [
            jnp.sum(prob_s, 0),
            jnp.sum(prob_t, 0),
            jnp.sum(prob_s * prob_s, 0),
            jnp.sum(prob_t * prob_t, 0),
            jnp.sum(prob_s * prob_t, 0),
        ]
    )
    sums = jnp.sum(spread(sums, SIDE, AXES, FIRST), 0)
    sums = jnp.sum(spread(sums, SIDE, AXES, SECOND), 0)
    mean_s = sums[0] / tokens
    mean_t = sums[1] / tokens
    col_var = sums[2] / tokens - mean_s * mean_s
    col_var_t = sums[3] / tokens - mean_t * mean_t
    col_cov = sums[4] / tokens - mean_s * mean_t
    col_den = jnp.sqrt((col_var + EPS) * (col_var_t + EPS))
    col_rho = col_cov / col_den

    inner = prob_t / row_den[:, None] - (row_rho / (row_var + EPS))[:, None] * prob_s
    inner = inner + (prob_t - mean_t[None, :]) / col_den[None, :]
    inner = inner - (col_rho / (col_var + EPS))[None, :] * (prob_s - mean_s[None, :])
    coeff = -TEMP * inner
    steps = tok_rows // TILE
    half = rows // CORES
    area = tok_rows * vocab_cols
    own_dot = jnp.sum(prob_s * coeff, 1)
    mean = own_dot / jnp.maximum(jnp.sum(prob_s, 1), 1e-30)
    shares = spread(own_dot[None], VOCAB, "vocab")
    tile = pl.BlockSpec((TILE, vocab_cols), lambda i: (i, 0))
    products = _call(
        product_kernel,
        steps,
        [
            pl.BlockSpec(memory_space=pltpu.SMEM),
            tile,
            tile,
            pl.BlockSpec((TILE, 1), lambda i: (i, 0)),
            pl.BlockSpec(near.shape, lambda i: (0, 0), pipeline_mode=pl.Buffered(1)),
            pl.BlockSpec(far.shape, lambda i: (0, 0), pipeline_mode=pl.Buffered(1)),
        ],
        pl.BlockSpec((2, CORES, DP, half, TILE), lambda i: (0, 0, 0, 0, i)),
        jax.ShapeDtypeStruct((2, CORES, DP, half, tok_rows), F32),
        [pltpu.VMEM((2 * TILE, vocab_cols), BF16), pltpu.VMEM((width, 2 * TILE), F32)],
        4 * area * width,
        16 * area,
    )(slot, _far(prob_s), _far(coeff), mean[:, None], _far(near), _far(far))
    row_dot = jnp.sum(shares, (0, 1)) / classes
    piece = jax.ShapeDtypeStruct((DP, half, tok_rows), F32)
    keep, send = _small(
        lambda *refs: shift_kernel(classes, *refs), [piece, piece], mean[None], shares, products
    )
    share = _small(
        add_kernel,
        jax.ShapeDtypeStruct((DP, half * steps, TILE), BF16),
        keep,
        lax.ppermute(send, "vocab", PAIR),
        scratch=[pltpu.VMEM((DP, half * steps, TILE), F32)],
    )
    share = lax.all_to_all(share, "vocab", 0, 0, tiled=True, axis_index_groups=COLUMN)
    logit_grad = (prob_s * (coeff - row_dot[:, None]) / TEMP).astype(BF16)
    hidden_grad = _small(last_kernel, jax.ShapeDtypeStruct((half, tok_rows), F32), share)
    return (logit_grad, hidden_grad.T.astype(BF16))


def solution(mesh):
    return jax.shard_map(
        body,
        mesh=mesh,
        in_specs=(P("dp", None), P("dp", "vocab"), P("dp", "vocab")),
        out_specs=(P("dp", "vocab"), P("dp", "vocab")),
        check_vma=False,
    )
```

```python
import jax
import jax.numpy as jnp
from jax import lax
from jax.experimental import pallas as pl
from jax.experimental.pallas import tpu as pltpu
from jax.sharding import PartitionSpec as P

TEMP = 4
EPS = 1e-06
SIDE = 4
CHIPS = 16
CORES = 2
DP = SIDE * SIDE
VOCAB = CHIPS * CORES
AXES = ("dp", "vocab")
TILE = 128
GRANT = 22 * 1024 * 1024
F32, BF16 = jnp.float32, jnp.bfloat16


def _step_pairs(step, second):
    pairs = []
    for x in range(SIDE):
        for y in range(SIDE):
            for v in range(VOCAB):
                along_x = (v % CORES == 0) != second
                tx, ty = ((x + step) % SIDE, y) if along_x else (x, (y + step) % SIDE)
                pairs.append(((x * SIDE + y) * VOCAB + v, (tx * SIDE + ty) * VOCAB + v))
    return pairs


OVER = [_step_pairs(step, False) for step in (1, SIDE - 1, 2)]
AHEAD, BACK = _step_pairs(1, True), _step_pairs(SIDE - 1, True)
COLUMN = [[z * CORES + core for z in range(CHIPS)] for core in range(CORES)]
PAIR = [(i, i ^ 1) for i in range(VOCAB)]


def spread(block, count, axis, groups=None):
    copies = jnp.broadcast_to(block[None], (count,) + block.shape)
    return lax.all_to_all(copies, axis, 0, 0, tiled=True, axis_index_groups=groups)


def _chunks(total, size):
    return [(at, min(at + size, total)) for at in range(0, total, size)]


def _rows(i, size):
    return pl.ds(pl.multiple_of(i * size, size), size)


def _loop(count, step, unroll):
    lax.fori_loop(0, count, lambda i, c: (step(i), c)[1], 0, unroll=unroll)


def product_kernel(place_ref, q_ref, g_ref, mean_ref, near_ref, far_ref, out_ref, left, res):
    def step(i):
        rows = _rows(i, 16)
        qs = q_ref[rows, :]
        left[rows, :] = (qs * (g_ref[rows, :] - mean_ref[rows, :]) * (1.0 / TEMP)).astype(BF16)
        left[pl.ds(pl.multiple_of(TILE + i * 16, 16), 16), :] = (qs * (1.0 / TEMP)).astype(BF16)

    _loop(TILE // 16, step, 2)
    cut = near_ref.shape[0]
    for part_ref, lo, hi in ((near_ref, 0, cut), (far_ref, cut, res.shape[0])):
        res[lo:hi] = lax.dot_general(
            part_ref[...], left[...], (((1,), (1,)), ((), ())), preferred_element_type=F32
        )
    half = out_ref.shape[3]
    for j in range(DP):
        for core in range(CORES):
            lo = (j * CORES + core) * half
            away = (place_ref[DP] + core) % CORES
            for k in range(2):
                out_ref[k, away, place_ref[j]] = res[lo : lo + half, k * TILE : (k + 1) * TILE]


def shift_kernel(classes, mean_ref, shares_ref, products_ref, keep_ref, send_ref):
    shift = mean_ref[...] - jnp.sum(shares_ref[:, 0, :], axis=0, keepdims=True) / classes
    for j in range(keep_ref.shape[0]):
        keep_ref[j] = products_ref[0, 0, j] + shift * products_ref[1, 0, j]
        send_ref[j] = products_ref[0, 1, j] + shift * products_ref[1, 1, j]


def add_kernel(a_ref, b_ref, out_ref, packed):
    half, tok = a_ref.shape[1:]
    for j in range(out_ref.shape[0]):
        for k in range(tok // TILE):
            at = slice(k * TILE, (k + 1) * TILE)
            packed[j, k * half : (k + 1) * half] = a_ref[j, :, at] + b_ref[j, :, at]
        out_ref[j] = packed[j].astype(BF16)


def last_kernel(share_ref, out_ref):
    half, tok = out_ref.shape
    total = share_ref[0].astype(F32)
    for j in range(1, share_ref.shape[0]):
        total = total + share_ref[j].astype(F32)
    for k in range(tok // TILE):
        out_ref[:, k * TILE : (k + 1) * TILE] = total[k * half : (k + 1) * half]


def _call(kernel, steps, in_specs, out_specs, out_shape, scratch, flops, nbytes):
    return pl.pallas_call(
        kernel,
        grid=(steps,),
        in_specs=in_specs,
        out_specs=out_specs,
        out_shape=out_shape,
        scratch_shapes=scratch,
        compiler_params=pltpu.CompilerParams(
            dimension_semantics=("arbitrary",), vmem_limit_bytes=GRANT
        ),
        cost_estimate=pl.CostEstimate(flops=flops, bytes_accessed=nbytes, transcendentals=0),
    )


def _far(x):
    return pltpu.with_memory_space_constraint(x, pltpu.HBM)


def _small(kernel, out_shape, *args, scratch=()):
    return pl.pallas_call(
        kernel,
        out_shape=out_shape,
        scratch_shapes=scratch,
        compiler_params=pltpu.CompilerParams(vmem_limit_bytes=GRANT),
        cost_estimate=pl.CostEstimate(flops=1000000, bytes_accessed=4000000, transcendentals=0),
    )(*args)


def merge(parts):
    peak_s, peak_t = jnp.max(parts[:, 0], 0), jnp.max(parts[:, 1], 0)
    ws, wt = jnp.exp(parts[:, 0] - peak_s), jnp.exp(parts[:, 1] - peak_t)
    return jnp.stack(
        [
            peak_s,
            peak_t,
            jnp.sum(parts[:, 2] * ws, 0),
            jnp.sum(parts[:, 3] * wt, 0),
            jnp.sum(parts[:, 4] * (ws * ws), 0),
            jnp.sum(parts[:, 5] * (wt * wt), 0),
            jnp.sum(parts[:, 6] * (ws * wt), 0),
        ]
    )


def body(student_hidden, head_weight, teacher_logits):
    tok_rows, width = student_hidden.shape
    rows, vocab_cols = head_weight.shape
    classes = vocab_cols * VOCAB
    tokens = tok_rows * DP
    core = lax.axis_index("vocab") % CORES

    behind, before, across = (lax.ppermute(head_weight, AXES, pairs) for pairs in OVER)

    mine = lax.axis_index("dp")
    down, right = mine // SIDE, mine % SIDE
    first = jnp.where(core == 0, down, right)
    second = jnp.where(core == 0, right, down)
    offsets = (0, SIDE - 1, 1, 2)
    hid = student_hidden.reshape(tok_rows, SIDE, SIDE, rows)
    hid = jnp.where(core == 0, jnp.swapaxes(hid, 1, 2), hid)
    hid = jnp.concatenate(
        [lax.dynamic_slice_in_dim(hid, (first + o) % SIDE, 1, 2) for o in offsets], 2
    ).reshape(tok_rows, SIDE, SIDE * rows)
    hid = [
        lax.dynamic_slice_in_dim(hid, (second + o) % SIDE, 1, 1).reshape(tok_rows, SIDE * rows)
        for o in offsets
    ]
    turn = jnp.stack([(second + offsets[k // SIDE]) % SIDE for k in range(DP)])
    along = jnp.stack([(first + offsets[k % SIDE]) % SIDE for k in range(DP)])
    slot = jnp.where(core == 0, along * SIDE + turn, turn * SIDE + along)
    slot = jnp.concatenate([slot, core[None]]).astype(jnp.int32)
    behind, hid_near, hid_far, slot = lax.optimization_barrier(
        (behind, jnp.concatenate(hid[:3], 1), hid[3], slot)
    )
    early = jnp.concatenate([head_weight, behind], 0)
    left_early = lax.ppermute(early, AXES, AHEAD)
    right_early = lax.ppermute(early, AXES, BACK)
    late = jnp.concatenate([before, across], 0)
    right_late = lax.ppermute(late, AXES, BACK)
    left_late = lax.ppermute(late, AXES, AHEAD)
    far = jnp.concatenate(
        [lax.ppermute(left_early, AXES, AHEAD), lax.ppermute(right_late, AXES, BACK)], 0
    )
    near = jnp.concatenate([early, late, left_early, left_late, right_early, right_late], 0)
    logits = jnp.dot(hid_near, near, preferred_element_type=F32)
    logits = logits + jnp.dot(hid_far, far, preferred_element_type=F32)
    scaled_student = logits / TEMP
    scaled_teacher = teacher_logits.astype(jnp.float32) / TEMP
    own_s = jnp.max(scaled_student, axis=1)
    own_t = jnp.max(scaled_teacher, axis=1)
    exp_s = jnp.exp(scaled_student - own_s[:, None])
    exp_t = jnp.exp(scaled_teacher - own_t[:, None])
    stats = jnp.stack(
        [
            own_s,
            own_t,
            jnp.sum(exp_s, 1),
            jnp.sum(exp_t, 1),
            jnp.sum(exp_s * exp_s, 1),
            jnp.sum(exp_t * exp_t, 1),
            jnp.sum(exp_s * exp_t, 1),
        ]
    )
    stats = merge(jnp.stack([stats, lax.ppermute(stats, "vocab", PAIR)]))
    stats = merge(spread(stats, CHIPS, "vocab", COLUMN))
    norm_s, norm_t = stats[2], stats[3]
    row_var = classes * stats[4] / (norm_s * norm_s) - 1.0
    row_var_t = classes * stats[5] / (norm_t * norm_t) - 1.0
    cross = classes * stats[6] / (norm_s * norm_t) - 1.0
    row_den = jnp.sqrt((row_var + EPS) * (row_var_t + EPS))
    row_rho = cross / row_den
    prob_s = exp_s * (classes * jnp.exp(own_s - stats[0]) / norm_s)[:, None]
    prob_t = exp_t * (classes * jnp.exp(own_t - stats[1]) / norm_t)[:, None]

    sums = jnp.stack(
        [
            jnp.sum(prob_s, 0),
            jnp.sum(prob_t, 0),
            jnp.sum(prob_s * prob_s, 0),
            jnp.sum(prob_t * prob_t, 0),
            jnp.sum(prob_s * prob_t, 0),
        ]
    )
    sums = jnp.sum(spread(sums, DP, "dp"), 0)
    mean_s = sums[0] / tokens
    mean_t = sums[1] / tokens
    col_var = sums[2] / tokens - mean_s * mean_s
    col_var_t = sums[3] / tokens - mean_t * mean_t
    col_cov = sums[4] / tokens - mean_s * mean_t
    col_den = jnp.sqrt((col_var + EPS) * (col_var_t + EPS))
    col_rho = col_cov / col_den

    inner = prob_t / row_den[:, None] - (row_rho / (row_var + EPS))[:, None] * prob_s
    inner = inner + (prob_t - mean_t[None, :]) / col_den[None, :]
    inner = inner - (col_rho / (col_var + EPS))[None, :] * (prob_s - mean_s[None, :])
    coeff = -TEMP * inner
    steps = tok_rows // TILE
    half = rows // CORES
    area = tok_rows * vocab_cols
    own_dot = jnp.sum(prob_s * coeff, 1)
    mean = own_dot / jnp.maximum(jnp.sum(prob_s, 1), 1e-30)
    shares = spread(own_dot[None], VOCAB, "vocab")
    tile = pl.BlockSpec((TILE, vocab_cols), lambda i: (i, 0))
    products = _call(
        product_kernel,
        steps,
        [
            pl.BlockSpec(memory_space=pltpu.SMEM),
            tile,
            tile,
            pl.BlockSpec((TILE, 1), lambda i: (i, 0)),
            pl.BlockSpec(near.shape, lambda i: (0, 0), pipeline_mode=pl.Buffered(1)),
            pl.BlockSpec(far.shape, lambda i: (0, 0), pipeline_mode=pl.Buffered(1)),
        ],
        pl.BlockSpec((2, CORES, DP, half, TILE), lambda i: (0, 0, 0, 0, i)),
        jax.ShapeDtypeStruct((2, CORES, DP, half, tok_rows), F32),
        [pltpu.VMEM((2 * TILE, vocab_cols), BF16), pltpu.VMEM((width, 2 * TILE), F32)],
        4 * area * width,
        16 * area,
    )(slot, _far(prob_s), _far(coeff), mean[:, None], _far(near), _far(far))
    row_dot = jnp.sum(shares, (0, 1)) / classes
    piece = jax.ShapeDtypeStruct((DP, half, tok_rows), F32)
    keep, send = _small(
        lambda *refs: shift_kernel(classes, *refs), [piece, piece], mean[None], shares, products
    )
    share = _small(
        add_kernel,
        jax.ShapeDtypeStruct((DP, half * steps, TILE), BF16),
        keep,
        lax.ppermute(send, "vocab", PAIR),
        scratch=[pltpu.VMEM((DP, half * steps, TILE), F32)],
    )
    share = lax.all_to_all(share, "vocab", 0, 0, tiled=True, axis_index_groups=COLUMN)
    logit_grad = (prob_s * (coeff - row_dot[:, None]) / TEMP).astype(BF16)
    hidden_grad = _small(last_kernel, jax.ShapeDtypeStruct((half, tok_rows), F32), share)
    return (logit_grad, hidden_grad.T.astype(BF16))


def solution(mesh):
    return jax.shard_map(
        body,
        mesh=mesh,
        in_specs=(P("dp", None), P("dp", "vocab"), P("dp", "vocab")),
        out_specs=(P("dp", "vocab"), P("dp", "vocab")),
        check_vma=False,
    )
```
